32 devices in a mesh: rep: 16 (over z, x, core), shard: 2 (over y).
Axes of the slice: x: 2, y: 2, z: 4, core: 2. Of those that a mesh axis runs over, the one named last changes fastest.
Arguments:
- images: bfloat16 [32, 577, 1024], P(('rep', 'shard')), may hold values from -6 to 6
- qkv_weight: bfloat16 [1024, 3072], P('shard'), may hold values from -0.1875 to 0.1875
- out_weight: bfloat16 [1024, 1024], P('shard'), may hold values from -2 to 2
- up_weight: bfloat16 [1024, 4096], P('shard'), may hold values from -0.1875 to 0.1875
- down_weight: bfloat16 [4096, 1024], P('shard'), may hold values from -0.09375 to 0.09375
- query_bias: bfloat16 [1024], P('shard'), may hold values from -1.796875 to 1.796875
- value_bias: bfloat16 [1024], P('shard'), may hold values from -1.796875 to 1.796875
- out_bias: bfloat16 [1024], P('shard'), may hold values from -1.796875 to 1.796875
- up_bias: bfloat16 [4096], P('shard'), may hold values from -1.796875 to 1.796875
- down_bias: bfloat16 [1024], P('shard'), may hold values from -1.796875 to 1.796875
- first_gain: bfloat16 [1024], P('shard'), may hold values from 0.5 to 1.5
- first_shift: bfloat16 [1024], P('shard'), may hold values from -1.796875 to 1.796875
- second_gain: bfloat16 [1024], P('shard'), may hold values from 0.5 to 1.5
- second_shift: bfloat16 [1024], P('shard'), may hold values from -1.796875 to 1.796875
- cotangent: bfloat16 [32, 577, 1024], P(('rep', 'shard')), may hold values from -6 to 6
Outputs:
- output: bfloat16 [32, 577, 1024], P(('rep', 'shard'))
- input_grad: float32 [32, 577, 1024], P(('rep', 'shard'))
- qkv_grad: float32 [1024, 3072], P('shard')
- out_grad: float32 [1024, 1024], P('shard')
- up_grad: float32 [1024, 4096], P('shard')
- down_grad: float32 [4096, 1024], P('shard')
- query_bias_grad: float32 [1024], P('shard')
- value_bias_grad: float32 [1024], P('shard')
- out_bias_grad: float32 [1024], P('shard')
- up_bias_grad: float32 [4096], P('shard')
- down_bias_grad: float32 [1024], P('shard')
- first_gain_grad: float32 [1024], P('shard')
- first_shift_grad: float32 [1024], P('shard')
- second_gain_grad: float32 [1024], P('shard')
- second_shift_grad: float32 [1024], P('shard')
The draws below stay inside these ranges and needn't reach their ends.
All inputs are finite; a program needn't handle non-finite values.
Results may differ from the reference program's by a relative error of at most 0.01.
Values may be sent and summed in bfloat16 or wider, within the bound.
No kernel may reach another device: no remote copies, remote signals or barrier semaphores. Data moves between devices by JAX's collectives and lax.ppermute only.
A program may use at most 256 MiB of HBM per device.

```python
import jax
import jax.numpy as jnp
from jax import lax

D = 1024
HEADS = 16
HEAD_DIM = 64
FF = 4096
SEQ = 577
IMAGES = 32


def levels(own_key, dims, split, low, top_value):
    level = 1.0
    for dim, parts in split:
        steps = jax.random.uniform(jax.random.fold_in(jax.random.fold_in(own_key, 6), dim), (parts,), jnp.float32, low / len(split), top_value / len(split))
        level = level * jnp.repeat(jnp.exp(steps), dims[dim] // parts).reshape((-1,) + (1,) * (len(dims) - 1 - dim))
    return level


def normal_values(own_key, extent, scale, reach, split=(), dtype=jnp.bfloat16):
    array = jax.random.normal(own_key, extent, jnp.float32) * scale
    if len(split) > 0:
        array = levels(own_key, extent, split, -0.22, 0.18) * array
    return jnp.clip(array, min=-reach, max=reach).astype(dtype)


def setup_inputs(seed: int = 0) -> dict:
    arg_keys = jax.random.split(jax.random.key(seed), 16)
    return {
        "images": normal_values(arg_keys[0], (IMAGES, SEQ, D), 1.0, 6.0, ((0, 32),)),
        "qkv_weight": normal_values(arg_keys[1], (D, 3 * D), D ** -0.5, 0.1875, ((0, 2),)),
        "out_weight": normal_values(arg_keys[2], (D, D), (max(D // 128, 4)) ** -0.5, 2.0, ((0, 2),)),
        "up_weight": normal_values(arg_keys[3], (D, FF), D ** -0.5, 0.1875, ((0, 2),)),
        "down_weight": normal_values(arg_keys[4], (FF, D), FF ** -0.5, 0.09375, ((0, 2),)),
        "query_bias": normal_values(arg_keys[5], (D,), 0.3, 1.796875, ((0, 2),)),
        "value_bias": normal_values(arg_keys[6], (D,), 0.3, 1.796875, ((0, 2),)),
        "out_bias": normal_values(arg_keys[7], (D,), 0.3, 1.796875, ((0, 2),)),
        "up_bias": normal_values(arg_keys[8], (FF,), 0.3, 1.796875, ((0, 2),)),
        "down_bias": normal_values(arg_keys[9], (D,), 0.3, 1.796875, ((0, 2),)),
        "first_gain": jnp.clip(1.0 + 0.1 * jax.random.normal(arg_keys[10], (D,), jnp.float32), 0.5, 1.5).astype(jnp.bfloat16),
        "first_shift": normal_values(arg_keys[11], (D,), 0.3, 1.796875, ((0, 2),)),
        "second_gain": jnp.clip(1.0 + 0.1 * jax.random.normal(arg_keys[12], (D,), jnp.float32), 0.5, 1.5).astype(jnp.bfloat16),
        "second_shift": normal_values(arg_keys[13], (D,), 0.3, 1.796875, ((0, 2),)),
        "cotangent": normal_values(arg_keys[14], (IMAGES, SEQ, D), 1.0, 6.0, ((0, 32),)),
    }


@jax.custom_vjp
def low(v):
    return lax.optimization_barrier(v.astype(jnp.bfloat16)).astype(jnp.float32)

@jax.custom_vjp
def low_back(v):
    return v

def low_keep(v):
    return (low(v), None)

def low_pass(kept, grad):
    return (grad,)

def back_keep(v):
    return (v, None)

def back_low(kept, grad):
    return (low(grad),)
low.defvjp(low_keep, low_pass)
low_back.defvjp(back_keep, back_low)

def mat(left, right):
    return jnp.dot(left, right, precision=lax.Precision.HIGHEST, preferred_element_type=jnp.float32)

def normalize(value, gain, shift):
    center = value - lax.optimization_barrier(jnp.mean(value, -1, keepdims=True))
    spread = lax.optimization_barrier(jnp.mean(center * center, -1, keepdims=True))
    return center * lax.rsqrt(spread + 1e-06) * gain + shift

def layer(tokens, qkv_weight, out_weight, up_weight, down_weight, query_bias, value_bias, out_bias, up_bias, down_bias, first_gain, first_shift, second_gain, second_shift):
    width = tokens.shape[-1]
    first = low(normalize(tokens, first_gain, first_shift))
    joined = mat(first, qkv_weight) + jnp.concatenate([query_bias, jnp.zeros((width,), jnp.float32), value_bias])
    joined = low(low_back(joined))
    query = joined[:, :width].reshape(SEQ, HEADS, HEAD_DIM)
    key = joined[:, width:2 * width].reshape(SEQ, HEADS, HEAD_DIM)
    value = joined[:, 2 * width:].reshape(SEQ, HEADS, HEAD_DIM)
    scores = jnp.einsum('qhe,khe->hqk', query, key, precision=lax.Precision.HIGHEST)
    scores = low_back(scores * 0.125)
    shifted = jnp.exp(scores - lax.optimization_barrier(jnp.max(scores, -1, keepdims=True)))
    probs = shifted / lax.optimization_barrier(jnp.sum(shifted, -1, keepdims=True))
    mixed = jnp.einsum('hqk,khe->qhe', low(probs), value, precision=lax.Precision.HIGHEST)
    mixed = low(low_back(mixed.reshape(SEQ, width)))
    resid = tokens + low_back(mat(mixed, out_weight) + out_bias)
    second = low(normalize(resid, second_gain, second_shift))
    hidden = low_back(mat(second, up_weight) + up_bias)
    active = low(jax.nn.gelu(hidden, approximate=False))
    return resid + mat(active, down_weight) + down_bias

def reference(images, qkv_weight, out_weight, up_weight, down_weight, query_bias, value_bias, out_bias, up_bias, down_bias, first_gain, first_shift, second_gain, second_shift, cotangent):
    params = tuple((w.astype(jnp.float32) for w in (qkv_weight, out_weight, up_weight, down_weight, query_bias, value_bias, out_bias, up_bias, down_bias, first_gain, first_shift, second_gain, second_shift)))

    def one_image(totals, item):
        tokens, grad_out = item
        result, backward = jax.vjp(layer, tokens.astype(jnp.float32), *params)
        grads = backward(grad_out.astype(jnp.float32))
        totals = tuple((a + b for a, b in zip(totals, grads[1:])))
        return (totals, (result.astype(jnp.bfloat16), grads[0]))
    zeros = tuple((jnp.zeros_like(w) for w in params))
    totals, (output, input_grad) = lax.scan(one_image, zeros, (images, cotangent))
    return (output, input_grad, totals[0], totals[1], totals[2], totals[3], totals[4], totals[5], totals[6], totals[7], totals[8], totals[9], totals[10], totals[11], totals[12])
```

```python
import functools
import jax
import jax.numpy as jnp
from jax import lax
from jax.experimental import pallas as pl
from jax.experimental.pallas import tpu as pltpu
from jax.sharding import Mesh
from jax.sharding import PartitionSpec as P

LANES = 128
VMEM_LIMIT = 48 * 1024 * 1024


def round_up(value, multiple):
    return -(-value // multiple) * multiple


def slabs(length):
    top = round_up(length, 16)
    return [(low, min(LANES, top - low)) for low in range(0, top, LANES)]


def contract(left, right, left_dim, right_dim):
    return lax.dot_general(
        left, right, (((left_dim,), (right_dim,)), ((), ())), preferred_element_type=jnp.float32
    )


def clean(ref, length):
    rows = lax.broadcasted_iota(jnp.int32, ref.shape, 0)
    return jnp.where(rows < length, ref[...], jnp.zeros(ref.shape, ref.dtype))


def attend_kernel(length, query_ref, key_ref, value_ref, mixed_ref, logsum_ref):
    query = clean(query_ref, length) * jnp.bfloat16(0.125)
    key = clean(key_ref, length)
    value_turned = jnp.transpose(clean(value_ref, length))
    first = lax.broadcasted_iota(jnp.int32, query.shape, 1) < LANES // 2
    half = LANES // 2
    turned = []
    for head in range(2):
        own_query = jnp.where(first if head == 0 else ~first, query, jnp.zeros_like(query))
        scores, largest = [], None
        for low, size in slabs(length):
            part = contract(key[low : low + size], own_query, 1, 1)
            if low + size > length:
                rows = lax.broadcasted_iota(jnp.int32, part.shape, 0) + low
                part = jnp.where(rows < length, part, -1e30)
            scores.append(part)
            top = jnp.max(part, 0, keepdims=True)
            largest = top if largest is None else jnp.maximum(largest, top)
        total, mixed = None, None
        for (low, size), part in zip(slabs(length), scores):
            shifted = jnp.exp(part - largest)
            added = jnp.sum(shifted, 0, keepdims=True)
            weighted = contract(
                value_turned[head * half : (head + 1) * half, low : low + size],
                shifted.astype(jnp.bfloat16), 1, 0,
            )
            total = added if total is None else total + added
            mixed = weighted if mixed is None else mixed + weighted
        turned.append(mixed * (1.0 / total))
        logsum_ref[0, head : head + 1, :] = largest + jnp.log(total)
    mixed_ref[...] = jnp.transpose(jnp.concatenate(turned, 0)).astype(jnp.bfloat16)


def attend(joined):
    length, width = joined.shape[0], joined.shape[1] // 3
    pairs, padded = width // LANES, round_up(length, LANES)
    block = lambda shift: pl.BlockSpec((padded, LANES), lambda i: (0, i + shift))
    return pl.pallas_call(
        functools.partial(attend_kernel, length),
        grid=(pairs,),
        in_specs=[block(0), block(pairs), block(2 * pairs)],
        out_specs=[block(0), pl.BlockSpec((1, 2, padded), lambda i: (i, 0, 0))],
        out_shape=[
            jax.ShapeDtypeStruct((length, width), jnp.bfloat16),
            jax.ShapeDtypeStruct((pairs, 2, padded), jnp.float32),
        ],
        compiler_params=pltpu.CompilerParams(vmem_limit_bytes=VMEM_LIMIT),
        cost_estimate=pl.CostEstimate(
            flops=16 * padded * padded * width, bytes_accessed=8 * length * width,
            transcendentals=padded * padded * 16,
        ),
        name="attend",
    )(joined, joined, joined)


def attend_back_kernel(
    length, query_ref, key_ref, value_ref, mixed_ref, grad_ref, logsum_ref, out_ref
):
    padded = query_ref.shape[0]
    query = clean(query_ref, length) * jnp.bfloat16(0.125)
    key = clean(key_ref, length)
    value = clean(value_ref, length)
    grad = clean(grad_ref, length)
    first = lax.broadcasted_iota(jnp.int32, query.shape, 1) < LANES // 2
    weighed = jnp.transpose(grad.astype(jnp.float32) * clean(mixed_ref, length).astype(jnp.float32))
    key_turned = jnp.transpose(key)
    zero = jnp.zeros_like(query)
    half = LANES // 2
    turned = []
    done = {}
    for head in range(2):
        mask = first if head == 0 else ~first
        own_query = jnp.where(mask, query, zero)
        own_grad = jnp.where(mask, grad, zero)
        delta = jnp.sum(weighed[head * half : (head + 1) * half], 0, keepdims=True)
        level = logsum_ref[0, head : head + 1, :]
        total = None
        for low, size in slabs(length):
            scores = contract(key[low : low + size], own_query, 1, 1)
            probs = jnp.exp(scores - level)
            if low + size > length:
                rows = lax.broadcasted_iota(jnp.int32, probs.shape, 0) + low
                probs = jnp.where(rows < length, probs, 0.0)
            dots = contract(value[low : low + size], own_grad, 1, 1)
            grad_scores = (probs * (dots - delta)).astype(jnp.bfloat16)
            done[head, low] = (
                contract(grad_scores, query, 1, 0),
                contract(probs.astype(jnp.bfloat16), grad, 1, 0),
            )
            part = contract(key_turned[head * half : (head + 1) * half, low : low + size], grad_scores, 1, 0)
            total = part if total is None else total + part
            if head == 1:
                side = lax.broadcasted_iota(jnp.int32, (size, LANES), 1) < half
                one, two = done[0, low], done[1, low]
                out_ref[1, low : low + size, :] = jnp.where(side, one[0], two[0]).astype(jnp.bfloat16)
                out_ref[2, low : low + size, :] = jnp.where(side, one[1], two[1]).astype(jnp.bfloat16)
        turned.append(total)
    both = jnp.transpose(jnp.concatenate(turned, 0)) * 0.125
    out_ref[0] = both.astype(jnp.bfloat16)


def attend_back(joined, mixed, grad, logsum):
    length, width = mixed.shape
    pairs, padded = width // LANES, round_up(length, LANES)
    block = lambda shift: pl.BlockSpec((padded, LANES), lambda i: (0, i + shift))
    return pl.pallas_call(
        functools.partial(attend_back_kernel, length),
        grid=(pairs,),
        in_specs=[
            block(0), block(pairs), block(2 * pairs), block(0), block(0),
            pl.BlockSpec((1, 2, padded), lambda i: (i, 0, 0)),
        ],
        out_specs=pl.BlockSpec((3, padded, LANES), lambda i: (0, 0, i)),
        out_shape=jax.ShapeDtypeStruct((3, length, width), jnp.bfloat16),
        compiler_params=pltpu.CompilerParams(vmem_limit_bytes=VMEM_LIMIT),
        cost_estimate=pl.CostEstimate(
            flops=40 * padded * padded * width, bytes_accessed=20 * length * width,
            transcendentals=padded * padded * 16,
        ),
        name="attend_back",
    )(joined, joined, joined, mixed, grad, logsum)


def dot(left, right, left_dim=1, right_dim=0):
    return contract(left, right, left_dim, right_dim)


def low(value):
    return value.astype(jnp.bfloat16)


def wide(value):
    return value.astype(jnp.float32)


def after(value, *others):
    return lax.optimization_barrier((value,) + others)[0]


def swap(value, axis):
    return lax.ppermute(value, axis, [(0, 1), (1, 0)])


def columns(value, start, size):
    return lax.dynamic_slice_in_dim(value, start, size, 1)


def rows(value, start, size):
    return lax.dynamic_slice_in_dim(value, start, size, 0)


def pair(own, other, second):
    return jnp.concatenate([jnp.where(second, other, own), jnp.where(second, own, other)])


def doubling(value, axis, size, keep):
    if size & (size - 1):
        return lax.psum(value, axis)
    step = 1
    while step < size:
        moved = lax.ppermute(value, axis, [(i, i ^ step) for i in range(size)])
        value = keep(wide(value) + wide(moved))
        step *= 2
    return value


def center(value):
    shifted = value - jnp.mean(value, -1, keepdims=True)
    inverse = lax.rsqrt(jnp.mean(shifted * shifted, -1, keepdims=True) + 1e-06)
    return shifted * inverse, inverse


def center_back(grad, gain, unit, inverse):
    scaled = grad * gain
    moved = scaled - jnp.mean(scaled, -1, keepdims=True)
    moved = moved - unit * jnp.mean(scaled * unit, -1, keepdims=True)
    return inverse * moved, jnp.sum(grad * unit, 0), jnp.sum(grad, 0)


def gather(weights, sizes):
    y_size = sizes["y"]
    if y_size != 2:
        return [lax.all_gather(w, "y", axis=0, tiled=True) for w in weights]
    here = {axis: lax.axis_index(axis) for axis in ("x", "c", "y")}
    fetched, gate = [], None
    for own in weights:
        size = own.shape[0] // 4
        block = rows(own, (here["c"] * 2 + here["x"]) * size, size)
        if gate is not None:
            block = after(block, gate)
        one = swap(block, "y")
        fetched.append(one)
        gate = one
    full = []
    for own, one in zip(weights, fetched):
        height, size = own.shape[0], own.shape[0] // 4
        two = swap(one, "x")
        far_one, far_two = swap(one, "c"), swap(two, "c")
        whole = jnp.zeros((2 * height, own.shape[1]), own.dtype)
        whole = lax.dynamic_update_slice(whole, own, (here["y"] * height, 0))
        for c_flip, x_flip, piece in ((0, 0, one), (0, 1, two), (1, 0, far_one), (1, 1, far_two)):
            spot = (here["c"] ^ c_flip) * 2 + (here["x"] ^ x_flip)
            whole = lax.dynamic_update_slice(
                whole, piece, ((1 - here["y"]) * height + spot * size, 0)
            )
        full.append(whole)
    return full


def reduce_weight(left, right, sizes, quick):
    here = {axis: lax.axis_index(axis) for axis in ("x", "c", "y")}
    y_size = sizes["y"]
    height = left.shape[1] // (2 * y_size)
    piece = lambda yi, ci: dot(columns(left, (yi * 2 + ci) * height, height), right, 0, 0)
    core, mine = here["c"], here["y"]
    if y_size == 2:
        far = swap(low(piece(1 - mine, 1 - core)), "c")
        sent = swap(low(piece(1 - mine, core) + wide(far)), "y")
        near = swap(low(piece(mine, 1 - core)), "c")
        kept = low(piece(mine, core) + wide(near) + wide(sent))
    else:
        moved = swap(jnp.stack([low(piece(i, 1 - core)) for i in range(y_size)]), "c")
        summed = jnp.stack([low(piece(i, core) + wide(moved[i])) for i in range(y_size)])
        kept = lax.psum_scatter(summed, "y", scatter_dimension=0, tiled=False)
    half = height // 2
    moved = swap(rows(kept, (1 - here["x"]) * half, half), "x")
    part = low(wide(rows(kept, here["x"] * half, half)) + wide(moved))
    if quick:
        part = doubling(part, "z", sizes["z"], low)
    else:
        part = lax.psum(part, "z")
    both = pair(part, swap(part, "x"), here["x"] == 1)
    return wide(pair(both, swap(both, "c"), core == 1))


def reduce_small(value, sizes):
    value = value.reshape(-1, LANES)
    for axis in ("c", "x", "z", "y"):
        value = doubling(value, axis, sizes[axis], wide)
    return value.reshape(-1)


def body(
    sizes,
    images,
    qkv_weight,
    out_weight,
    up_weight,
    down_weight,
    query_bias,
    value_bias,
    out_bias,
    up_bias,
    down_bias,
    first_gain,
    first_shift,
    second_gain,
    second_shift,
    cotangent,
):
    batch, length, width = images.shape
    vectors = (
        query_bias, value_bias, out_bias, up_bias, down_bias,
        first_gain, first_shift, second_gain, second_shift,
    )
    packed = lax.all_gather(jnp.concatenate(vectors), "y", axis=0, tiled=False)
    spread, start = [], 0
    for vector in vectors:
        spread.append(wide(packed[:, start : start + vector.shape[0]].reshape(-1)))
        start += vector.shape[0]
    (
        query_bias, value_bias, out_bias, up_bias, down_bias,
        first_gain, first_shift, second_gain, second_shift,
    ) = spread
    qkv_full, out_full, up_full, down_full = gather(
        [qkv_weight, out_weight, up_weight, down_weight], sizes
    )
    tokens = wide(images.reshape(batch * length, width))
    grad_out = cotangent.reshape(batch * length, width)
    unit_one, inverse_one = center(tokens)
    first = low(unit_one * first_gain + first_shift)
    joined_bias = jnp.concatenate([query_bias, jnp.zeros_like(query_bias), value_bias])
    joined = low(dot(first, qkv_full) + joined_bias)
    split = lambda value: [value[i * length : (i + 1) * length] for i in range(batch)]
    attended = [attend(item) for item in split(joined)]
    mixed = jnp.concatenate([item[0] for item in attended])
    resid = tokens + dot(mixed, out_full) + out_bias
    unit_two, inverse_two = center(resid)
    second = low(unit_two * second_gain + second_shift)
    hidden = dot(second, up_full) + up_bias
    below = 0.5 + 0.5 * lax.erf(hidden * (0.5**0.5))
    density = jnp.exp(-0.5 * hidden * hidden) * (1.0 / (2.0 * 3.141592653589793) ** 0.5)
    active, slope = lax.optimization_barrier((low(hidden * below), below + hidden * density))
    down_grad = reduce_weight(active, grad_out, sizes, False)
    down_bias_grad = jnp.sum(wide(grad_out), 0)
    grad_hidden = low(dot(grad_out, down_full, 1, 1) * slope)
    up_grad = reduce_weight(second, grad_hidden, sizes, False)
    up_bias_grad = jnp.sum(wide(grad_hidden), 0)
    grad_second = dot(grad_hidden, up_full, 1, 1)
    moved, second_gain_grad, second_shift_grad = center_back(
        grad_second, second_gain, unit_two, inverse_two
    )
    grad_resid = wide(grad_out) + moved
    grad_attn = low(grad_resid)
    out_grad = reduce_weight(mixed, grad_attn, sizes, False)
    out_bias_grad = jnp.sum(wide(grad_attn), 0)
    grad_mixed = low(dot(grad_attn, out_full, 1, 1))
    backs = [
        attend_back(item, own, grad, kept[1])
        for item, own, grad, kept in zip(split(joined), split(mixed), split(grad_mixed), attended)
    ]
    grad_joined = jnp.concatenate(
        [jnp.concatenate([back[i] for i in range(3)], -1) for back in backs]
    )
    qkv_grad = reduce_weight(first, grad_joined, sizes, True)
    bias_sums = jnp.sum(wide(grad_joined), 0)
    grad_first = dot(grad_joined, qkv_full, 1, 1)
    moved, first_gain_grad, first_shift_grad = center_back(
        grad_first, first_gain, unit_one, inverse_one
    )
    input_grad = grad_resid + moved
    output = low(resid + dot(active, down_full) + down_bias)
    small = (
        bias_sums[:width], bias_sums[2 * width :], out_bias_grad, up_bias_grad, down_bias_grad,
        first_gain_grad, first_shift_grad, second_gain_grad, second_shift_grad,
    )
    y_size, y_index = sizes["y"], lax.axis_index("y")
    summed = reduce_small(jnp.concatenate(small), sizes)
    owned, start = [], 0
    for vector in small:
        size = vector.shape[0] // y_size
        owned.append(lax.dynamic_slice_in_dim(summed, start + y_index * size, size))
        start += vector.shape[0]
    shape = (batch, length, width)
    return (
        output.reshape(shape), input_grad.reshape(shape),
        qkv_grad, out_grad, up_grad, down_grad, *owned,
    )


def solution(mesh):
    rep, shard = mesh.shape["rep"], mesh.shape["shard"]
    sizes = {"z": rep // 4, "x": 2, "c": 2, "y": shard}
    fine = Mesh(mesh.devices.reshape(tuple(sizes.values())), tuple(sizes))
    whole = P(("z", "x", "c", "y"), None, None)
    matrix, vector = P("y", None), P("y")
    return jax.shard_map(
        functools.partial(body, sizes),
        mesh=fine,
        in_specs=(whole,) + (matrix,) * 4 + (vector,) * 9 + (whole,),
        out_specs=(whole, whole) + (matrix,) * 4 + (vector,) * 9,
        check_vma=False,
    )
```
